1024 devices in a mesh: dp: 32 (over z, y_hi, core), expert: 32 (over x, y_lo).
Axes of the slice: x: 8, y: 8 (y_hi: 2, y_lo: 4; y = y_hi * 4 + y_lo), z: 8, core: 2. Of those that a mesh axis runs over, the one named last changes fastest.
Arguments:
- tokens: bfloat16 [4096, 3584], P(('dp', 'expert')), may hold values from -6 to 6
- routes: int32 [4096, 2], P(('dp', 'expert')), may hold values from 0 to 3, all different within a row; in each aligned block of 4 rows (0 to 3, 4 to 7, ...) at most 4 rows name the same one
- route_gates: float32 [4096, 2], P(('dp', 'expert')), may hold values from 0.1 to 0.6
- out_grad: bfloat16 [4096, 3584], P(('dp', 'expert')), may hold values from -6 to 6
- w_gate: bfloat16 [3584, 4096], P(None, 'expert'), may hold values from -0.09375 to 0.09375
- w_up: bfloat16 [3584, 4096], P(None, 'expert'), may hold values from -0.09375 to 0.09375
- w_down: bfloat16 [4096, 3584], P('expert'), may hold values from -0.1875 to 0.1875
Outputs:
- moe_out: bfloat16 [4096, 3584], P(('dp', 'expert'))
- token_grad: bfloat16 [4096, 3584], P(('dp', 'expert'))
- grad_gate: bfloat16 [3584, 4096], P('dp', 'expert')
- grad_up: bfloat16 [3584, 4096], P('dp', 'expert')
- grad_down: bfloat16 [4096, 3584], P('expert', 'dp')
The draws below stay inside these ranges and needn't reach their ends.
Inputs may be any that keep to these rules, and one draw needn't show every extreme that they name: `routes`: each row names 2 different experts; among the rows of one device no expert is named by more than 4 rows, a bound that some block reaches.
All inputs are finite; a program needn't handle non-finite values.
Results may differ from the reference program's by a relative error of at most 0.02.
Values may be sent and summed in bfloat16 or wider, within the bound.
A program may use at most 32 MiB of HBM per device.

```python
import math
import jax
import jax.numpy as jnp
import numpy as np
from jax import lax

D = 3584
FF_WIN = 1024
TOK_DEV = 4
SLICES = 8
FF_DEV = 128
EXPERTS = 4
TOPK = 2
CAP = 4
TOKENS = 4096
N_EXPERT = 32


def levels(rng, dims, pieces, smallest, top_value):
    def one(axis_at, parts):
        steps = jax.random.uniform(jax.random.fold_in(jax.random.fold_in(rng, 6), axis_at), (parts,), jnp.float32, smallest / len(pieces), top_value / len(pieces))
        return jnp.repeat(jnp.exp(steps), dims[axis_at] // parts).reshape((-1,) + (1,) * (len(dims) - axis_at - 1))

    factor_of = one(*pieces[0])
    for cut in pieces[1:]:
        factor_of = factor_of * one(*cut)
    return factor_of


def shared_out(own_key, own, number, rows, count, top, limit, skew):
    order = jax.random.permutation(own_key, count)
    packed, common = shares(count, rows * top, limit, skew, True), shares(count, rows * top, limit, skew, False)
    places = jnp.arange(count)

    def named(lengths, rotation):
        used = int((lengths > 0).sum())
        fixed = max(1, used // 4)
        moved = fixed + (places - fixed + rotation * (used - fixed)) % max(1, count - fixed)
        return jnp.zeros((count,), jnp.int32).at[order[jnp.where(places < fixed, places, moved)]].set(jnp.asarray(lengths, jnp.int32))

    lengths = jnp.where(number % 4 == 0, named(packed, number // 4), named(common, number - number // 4 - 1))
    mixed = jax.random.permutation(jax.random.fold_in(own, 3), count)
    giver, receiver = mixed[0:count // 2 * 2:2], mixed[1:count // 2 * 2:2]
    slack = jnp.minimum(lengths[giver] - 1, limit - lengths[receiver]) // 2
    slack = jnp.where((giver == order[0]) | (receiver == order[0]) | (lengths[receiver] == 0), 0, jnp.maximum(slack, 0))
    moved = jax.random.randint(jax.random.fold_in(own, 4), (count // 2,), 0, 1 << 20) % (slack + 1)
    lengths = lengths.at[giver].add(-moved).at[receiver].add(moved)
    labels = jnp.searchsorted(jnp.cumsum(lengths), jnp.arange(rows * top), side="right").astype(jnp.int32)
    grid = labels.reshape(top, rows).T
    grid = grid[jax.random.permutation(jax.random.fold_in(own, 1), rows)]
    rotation = jax.random.randint(jax.random.fold_in(own, 2), (rows, 1), 0, top)
    return jnp.take_along_axis(grid, (jnp.arange(top)[None, :] + rotation) % top, axis=1)


def shares(amount, total, reach, lean, full):
    loads = [(1 << 20) // math.isqrt(rank ** lean) + 1 for rank in range(1, amount + 1)]
    largest = reach if full else min(reach, max(-(-total // amount), total * loads[0] // sum(loads)))
    least = 1 if total - largest >= amount - 1 else 0
    holding, spare = [largest] + [least] * (amount - 1), total - largest - least * (amount - 1)
    while spare > 0:
        candidates = [i for i in range(1, amount) if holding[i] < largest] or [i for i in range(1, amount) if holding[i] < reach]
        whole, left = sum([loads[i] for i in candidates]), spare
        for i in candidates:
            addition = min(reach - holding[i], max(1, left * loads[i] // whole), spare)
            holding[i] = holding[i] + addition
            spare = spare - addition
    return np.array(holding)


def bell_draw(key, shape, width, limit, shards=(), held_as=jnp.bfloat16):
    values = width * jax.random.normal(key, shape, jnp.float32)
    if shards:
        values = values * levels(key, shape, shards, -0.22, 0.18)
    return jnp.clip(values, -limit, limit).astype(held_as)


def setup_inputs(seed: int = 0) -> dict:
    key_list = jax.random.split(jax.random.key(seed), 8)
    tokens = bell_draw(key_list[0], (TOKENS, D), 1.0, 6.0, ((0, 1024),))
    routes_keys = jax.random.split(jax.random.fold_in(key_list[1], 1), TOKENS // TOK_DEV)
    routes_turns = jax.random.permutation(jax.random.fold_in(key_list[1], 3), TOKENS // TOK_DEV)
    routes = jax.vmap(lambda own, number: shared_out(jax.random.fold_in(key_list[1], 2), own, number, TOK_DEV, EXPERTS, TOPK, CAP, 2))(routes_keys, routes_turns).reshape((TOKENS, TOPK))
    route_gates = jnp.clip(0.1 + 0.5 * jax.random.uniform(key_list[2], (TOKENS, TOPK), jnp.float32) ** levels(key_list[2], (TOKENS, TOPK), ((0, 1024),), -0.2, 0.2), 0.1, 0.6)
    out_grad = bell_draw(key_list[3], (TOKENS, D), 1.0, 6.0, ((0, 1024),))
    w_gate = bell_draw(key_list[4], (D, EXPERTS * FF_WIN), D ** -0.5, 0.09375, ((1, 32),))
    w_up = bell_draw(key_list[5], (D, EXPERTS * FF_WIN), D ** -0.5, 0.09375, ((1, 32),))
    w_down = bell_draw(key_list[6], (EXPERTS * FF_WIN, D), FF_WIN ** -0.5, 0.1875, ((0, 32),))
    return {"tokens": tokens, "routes": routes, "route_gates": route_gates, "out_grad": out_grad, "w_gate": w_gate, "w_up": w_up, "w_down": w_down}


def expert_pass(rows, slot_grad, wg, wu, wd):
    a = jnp.dot(rows, wg, preferred_element_type=jnp.float32)
    b = jnp.dot(rows, wu, preferred_element_type=jnp.float32)
    sig = jax.nn.sigmoid(a)
    act = a * sig
    hidden = (act * b).astype(jnp.bfloat16)
    out = jnp.dot(hidden, wd, preferred_element_type=jnp.float32).astype(jnp.bfloat16)
    d_hidden = jnp.dot(slot_grad, wd.T, preferred_element_type=jnp.float32)
    d_up = (d_hidden * act).astype(jnp.bfloat16)
    d_gate = (d_hidden * b * sig * (1.0 + a * (1.0 - sig))).astype(jnp.bfloat16)
    d_rows = (jnp.dot(d_gate, wg.T, preferred_element_type=jnp.float32) + jnp.dot(d_up, wu.T, preferred_element_type=jnp.float32)).astype(jnp.bfloat16)
    part_gate = jnp.dot(rows.T, d_gate, preferred_element_type=jnp.float32).astype(jnp.bfloat16).astype(jnp.float32)
    part_up = jnp.dot(rows.T, d_up, preferred_element_type=jnp.float32).astype(jnp.bfloat16).astype(jnp.float32)
    part_down = jnp.dot(hidden.T, slot_grad, preferred_element_type=jnp.float32).astype(jnp.bfloat16).astype(jnp.float32)
    return out, d_rows, part_gate, part_up, part_down


def reference(tokens, routes, route_gates, out_grad, w_gate, w_up, w_down):
    group_rows = TOK_DEV * N_EXPERT
    rows_cap = N_EXPERT * CAP
    groups = TOKENS // group_rows
    xg = tokens.reshape(groups, group_rows, D)
    rg = routes.reshape(groups, group_rows, TOPK)
    gg = route_gates.reshape(groups, group_rows, TOPK)
    dg = out_grad.reshape(groups, group_rows, D)
    wg4 = w_gate.reshape(D, EXPERTS, SLICES, FF_DEV).transpose(1, 2, 0, 3)
    wu4 = w_up.reshape(D, EXPERTS, SLICES, FF_DEV).transpose(1, 2, 0, 3)
    wd4 = w_down.reshape(EXPERTS, SLICES, FF_DEV, D)

    def group_step(carry, inputs):
        xgr, rgr, ggr, dgr = inputs

        def per_expert(expert_id):
            hit = rgr == expert_id
            chosen = jnp.any(hit, axis=1)
            gate = jnp.sum(jnp.where(hit, ggr, jnp.float32(0.0)), axis=1)
            iota = jnp.arange(group_rows, dtype=jnp.int32)
            keys = jnp.where(chosen, iota, iota + group_rows)
            order = jnp.argsort(keys)[:rows_cap].astype(jnp.int32)
            valid = chosen[order]
            gate_rows = jnp.where(valid, gate[order], jnp.float32(0.0))
            rows = xgr[order]
            slot_grad = (gate_rows[:, None] * dgr[order].astype(jnp.float32)).astype(jnp.bfloat16)

            def per_slice(slice_id):
                return expert_pass(rows, slot_grad, wg4[expert_id, slice_id], wu4[expert_id, slice_id], wd4[expert_id, slice_id])

            outs, drows, pg, pu, pd = lax.map(per_slice, jnp.arange(SLICES, dtype=jnp.int32))
            back_out = gate_rows[:, None] * jnp.sum(outs.astype(jnp.float32), axis=0)
            back_dx = jnp.where(valid[:, None], jnp.sum(drows.astype(jnp.float32), axis=0), jnp.float32(0.0))
            return order, back_out, back_dx, pg, pu, pd

        orders, back_out, back_dx, pg, pu, pd = lax.map(per_expert, jnp.arange(EXPERTS, dtype=jnp.int32))
        flat = orders.reshape(-1)
        tok_out = jnp.zeros((group_rows, D), jnp.float32).at[flat].add(back_out.reshape(-1, D))
        tok_dx = jnp.zeros((group_rows, D), jnp.float32).at[flat].add(back_dx.reshape(-1, D))
        return (carry[0] + pg, carry[1] + pu, carry[2] + pd), (tok_out, tok_dx)

    start = (jnp.zeros((EXPERTS, SLICES, D, FF_DEV), jnp.float32), jnp.zeros((EXPERTS, SLICES, D, FF_DEV), jnp.float32), jnp.zeros((EXPERTS, SLICES, FF_DEV, D), jnp.float32))
    sums, (outs, dxs) = lax.scan(group_step, start, (xg, rg, gg, dg))
    moe_out = outs.reshape(TOKENS, D).astype(jnp.bfloat16)
    token_grad = dxs.reshape(TOKENS, D).astype(jnp.bfloat16)
    grad_gate = sums[0].transpose(2, 0, 1, 3).reshape(D, EXPERTS * FF_WIN).astype(jnp.bfloat16)
    grad_up = sums[1].transpose(2, 0, 1, 3).reshape(D, EXPERTS * FF_WIN).astype(jnp.bfloat16)
    grad_down = sums[2].reshape(EXPERTS * FF_WIN, D).astype(jnp.bfloat16)
    return moe_out, token_grad, grad_gate, grad_up, grad_down
```

```python
import jax
import jax.numpy as jnp
from jax import lax
from jax.experimental import pallas as pl
from jax.experimental.pallas import tpu as pltpu
from jax.sharding import PartitionSpec as P

NX, NY, NZ, NH, NC = 8, 4, 8, 2, 2
EXPERTS = 4
SEG = 4
NB = 4
BF, F32 = jnp.bfloat16, jnp.float32
NN, NT, TN = (((1,), (0,)), ((), ())), (((1,), (1,)), ((), ())), (((0,), (0,)), ((), ()))


def mm(a, b, dims=NN, precision=None):
    return lax.dot_general(a, b, dims, precision=precision, preferred_element_type=F32)


def iota(shape, dim):
    return lax.broadcasted_iota(jnp.int32, shape, dim)


def split(n, tile):
    return -(-(n // tile) // 2) * tile


def build(tok, d, ff):
    lt, le = tok.bit_length() - 1, EXPERTS.bit_length() - 1
    ly = NY.bit_length() - 1
    seg_w = d // SEG
    chunk = SEG * tok
    brow = NY * tok
    rows = NX * brow
    hx, hz = NX // 2, NZ // 2
    bw, zb = d // NB, NZ // NB
    dr = d // (NZ * NH * NC)
    gr = 3 * dr
    ds = split(d, 128)
    gs = split(gr, 16)
    kb = 512
    n_copies = 9 * NY + 5 * 2 * hx + NB + 2 * 2 * hz + 4

    def kernel(
        tok_ref, routes_ref, gates_ref, og_ref, wg_hbm, wu_hbm, wd_hbm,
        out_ref, dx_ref, gg_ref, gu_ref, gd_ref,
        wgu, wd, xc, dc, gc, xy, dy, gy, xg, dg, gx, sdo,
        o_part, d_part, o_in, d_in, oc, xo, oy, xdy,
        gp, gcin, zsum, zin, hout, hin,
        wsem, ssem, rsem,
    ):
        dp, ei = lax.axis_index("dp"), lax.axis_index("expert")
        x, y = ei // NY, ei % NY
        z, h, c = dp // (NH * NC), (dp // NC) % NH, dp % NC

        def at_x(v):
            return (dp, v * NY + y)

        def at_y(v):
            return (dp, x * NY + v)

        def at_z(v):
            return ((v * NH + h) * NC + c, ei)

        right, left = at_x((x + 1) % NX), at_x((x + NX - 1) % NX)
        up, down = at_z((z + 1) % NZ), at_z((z + NZ - 1) % NZ)
        other_h = ((z * NH + 1 - h) * NC + c, ei)
        other_c = ((z * NH + h) * NC + 1 - c, ei)
        partners = [at_y((y + k) % NY) for k in range(1, NY)]
        partners += [right, left, up, down, other_h, other_c]

        barrier = pltpu.get_barrier_semaphore()
        for p in partners:
            pl.semaphore_signal(barrier, inc=1, device_id=p, device_id_type=pl.DeviceIdType.MESH)

        loads = [
            pltpu.make_async_copy(wg_hbm, wgu.at[:, 0:ff], wsem.at[0]),
            pltpu.make_async_copy(wu_hbm, wgu.at[:, ff : 2 * ff], wsem.at[1]),
            pltpu.make_async_copy(wd_hbm, wd, wsem.at[2]),
        ]
        for load in loads:
            load.start()

        sent = []
        ids = {}

        def copy(key, src, dst, dev):
            n = ids.setdefault(key, len(ids))
            return pltpu.make_async_remote_copy(
                src_ref=src, dst_ref=dst, send_sem=ssem.at[n], recv_sem=rsem.at[n],
                device_id=dev, device_id_type=pl.DeviceIdType.MESH,
            )

        def send(key, src, dst, dev):
            op = copy(key, src, dst, dev)
            op.start()
            sent.append(op)

        def arrive(key, dst, dev):
            copy(key, dst, dst, dev).wait_recv()

        def pack(ref):
            total = None
            for s in range(SEG):
                place = (iota((chunk, tok), 0) == iota((chunk, tok), 1) + s * tok).astype(BF)
                term = mm(place, ref[:, s * seg_w : (s + 1) * seg_w])
                total = term if total is None else total + term
            return total.astype(BF)

        xc[...] = pack(tok_ref)
        lane, row = iota((tok, 128), 1), iota((tok, 128), 0)
        table = jnp.zeros((tok, 128), F32)
        for k in range(routes_ref.shape[1]):
            mine = ((lane >> le) == row) & ((lane & (EXPERTS - 1)) == routes_ref[:, k : k + 1])
            table = table + jnp.where(mine, gates_ref[:, k : k + 1], 0.0)
        line = jnp.sum(table, axis=0, keepdims=True)
        gc[...] = jnp.where(iota((8, 128), 0) == y, line, 0.0)

        pl.semaphore_wait(barrier, len(partners))

        for k in range(1, NY):
            send(("yx", k), xc, xy.at[y], at_y((y + k) % NY))
        for k in range(1, NY):
            send(("yg", k), gc, gy.at[y], at_y((y + k) % NY))
        dc[...] = pack(og_ref)
        for k in range(1, NY):
            send(("yd", k), dc, dy.at[y], at_y((y + k) % NY))

        def place_of(s):
            r, q = iota((brow, NY * chunk), 0), iota((brow, NY * chunk), 1)
            return (q == (r >> lt) * chunk + s * tok + (r & (tok - 1))).astype(BF)

        def xrows(v):
            return pl.ds(pl.multiple_of((v % NX) * brow, brow), brow)

        def unpack_to(buf, own, dst):
            buf[pl.ds(y, 1)] = own[...][None]
            all_rows = buf[...].reshape(NY * chunk, seg_w)
            for s in range(SEG):
                dst[xrows(x), s * seg_w : (s + 1) * seg_w] = mm(place_of(s), all_rows).astype(BF)

        def gather_views(name, s):
            buf = {"x": xg, "d": dg}[name]
            r_cols, l_cols = (slice(0, ds), slice(ds, d)) if s == hx else (slice(0, d), slice(0, d))
            return buf, r_cols, l_cols

        def gather_send(name, s):
            buf, rc, lc = gather_views(name, s)
            v = buf.at[xrows(x + NX - s + 1), rc]
            send((name, "r", s), v, v, right)
            v = buf.at[xrows(x + s - 1), lc]
            send((name, "l", s), v, v, left)

        def gather_arrive(name, s):
            buf, rc, lc = gather_views(name, s)
            arrive((name, "r", s), buf.at[xrows(x + NX - s), rc], right)
            arrive((name, "l", s), buf.at[xrows(x + s), lc], left)

        def gate_send(s):
            v = gx.at[(x + NX - s + 1) % NX]
            send(("g", "r", s), v, v, right)
            if s < hx:
                v = gx.at[(x + s - 1) % NX]
                send(("g", "l", s), v, v, left)

        def gate_arrive(s):
            arrive(("g", "r", s), gx.at[(x + NX - s) % NX], right)
            if s < hx:
                arrive(("g", "l", s), gx.at[(x + s) % NX], left)

        for k in range(1, NY):
            arrive(("yx", k), xy.at[(y + NY - k) % NY], at_y((y + k) % NY))
        unpack_to(xy, xc, xg)
        gather_send("x", 1)
        for k in range(1, NY):
            arrive(("yg", k), gy.at[(y + NY - k) % NY], at_y((y + k) % NY))
        gy[pl.ds(y, 1)] = gc[...][None]
        gx[pl.ds(x, 1)] = jnp.sum(gy[...], axis=0, keepdims=True)
        gate_send(1)
        for k in range(1, NY):
            arrive(("yd", k), dy.at[(y + NY - k) % NY], at_y((y + k) % NY))
        unpack_to(dy, dc, dg)
        gather_send("d", 1)
        for s in range(1, hx):
            gather_arrive("x", s)
            gather_send("x", s + 1)
            gate_arrive(s)
            gate_send(s + 1)
            gather_arrive("d", s)
            gather_send("d", s + 1)
        gather_arrive("x", hx)
        gate_arrive(hx)

        expert = ei // (NX * NY // EXPERTS)
        t, q = iota((rows, NX * 8), 0), iota((rows, NX * 8), 1)
        pick = (q == (t >> (lt + ly)) * 8 + ((t >> lt) & (NY - 1))).astype(F32)
        picked = mm(pick, gx[...].reshape(NX * 8, 128), precision=lax.Precision.HIGHEST)
        t, q = iota((rows, 128), 0), iota((rows, 128), 1)
        mine = q == (t & (tok - 1)) * EXPERTS + expert
        gate = jnp.sum(jnp.where(mine, picked, 0.0), axis=1, keepdims=True)

        loads[0].wait()
        loads[1].wait()
        ab = jnp.zeros((rows, 2 * ff), F32)
        for i in range(0, d, kb):
            ab = ab + mm(xg[:, i : i + kb], wgu[i : i + kb, :])
        a, b = ab[:, 0:ff], ab[:, ff : 2 * ff]
        sig = jax.nn.sigmoid(a)
        act = a * sig
        hidden = (act * b).astype(BF)
        loads[2].wait()
        for i in range(0, d, kb):
            o_part[:, i : i + kb] = (mm(hidden, wd[:, i : i + kb]) * gate).astype(BF)

        def scatter_start(name, part, into):
            v = part.at[xrows(x + hx), 0:ds]
            send((name, "r", 1), v, into.at[0, 0, :, 0:ds], right)
            v = part.at[xrows(x + hx), ds:d]
            send((name, "l", 1), v, into.at[1, 0, :, ds:d], left)

        def scatter_step(name, part, into, s):
            for i, (way, dev) in enumerate((("r", right), ("l", left))):
                cols = slice(0, d) if s > 1 else slice(ds, d) if i else slice(0, ds)
                arrive((name, way, s), into.at[i, s - 1, :, cols], dev)
                at = xrows(x + hx - s) if i == 0 else xrows(x + NX - hx + s)
                total = part[at, cols].astype(F32) + into[i, s - 1, :, cols].astype(F32)
                part[at, cols] = total.astype(BF)
                send((name, way, s + 1), part.at[at], into.at[i, s], dev)

        def scatter_end(name, part, into):
            arrive((name, "r", hx), into.at[0, hx - 1], right)
            arrive((name, "l", hx), into.at[1, hx - 1], left)
            total = part[xrows(x), :].astype(F32) + into[0, hx - 1].astype(F32)
            return (total + into[1, hx - 1].astype(F32)).astype(BF)

        scatter_start("o", o_part, o_in)

        gather_arrive("d", hx)
        dh = jnp.zeros((rows, ff), F32)
        for i in range(0, d, kb):
            v = (dg[:, i : i + kb].astype(F32) * gate).astype(BF)
            sdo[:, i : i + kb] = v
            dh = dh + mm(v, wd[:, i : i + kb], NT)
        d_up = (dh * act).astype(BF)
        d_gate = (dh * b * sig * (1.0 + a * (1.0 - sig))).astype(BF)
        dgu = jnp.concatenate([d_gate, d_up], axis=1)

        order = [NB // 2, *(v for k in range(1, NB // 2) for v in (k, NB - k)), 0]

        def core_views(k):
            zs = pl.ds(((z // zb + order[k]) % NB) * zb, zb)
            return zs, gcin.at[zs]

        for k in range(NB):
            block = (z // zb + order[k]) % NB
            cols = pl.ds(pl.multiple_of(block * bw, bw), bw)
            pgu = mm(xg[:, cols], dgu, TN).astype(BF)
            pd = mm(sdo[:, cols], hidden, TN).astype(BF)
            for zz in range(zb):
                for hh in range(NH):
                    for cc in range(NC):
                        at = slice(((zz * NH + hh) * NC + cc) * dr, ((zz * NH + hh) * NC + cc + 1) * dr)
                        gp[cc, block * zb + zz, hh, 0:dr] = pgu[at, 0:ff]
                        gp[cc, block * zb + zz, hh, dr : 2 * dr] = pgu[at, ff : 2 * ff]
                        gp[cc, block * zb + zz, hh, 2 * dr : gr] = pd[at]
            zs, dst = core_views(k)
            send(("c", k), gp.at[1 - c, zs], dst, other_c)

        for i in range(0, d, kb):
            d_part[:, i : i + kb] = mm(dgu, wgu[i : i + kb, :], NT).astype(BF)
        scatter_start("dx", d_part, d_in)

        def both(zd, hh, at):
            return gp[c, zd, hh, at].astype(F32) + gcin[zd, hh, at].astype(F32)

        every, low, high = slice(0, gr), slice(0, gs), slice(gs, gr)

        def z_start(k, hh):
            zd = (z + hz) % NZ
            zsum[zd, hh] = both(zd, hh, every).astype(BF)
            send(("z", k, "u", 1), zsum.at[zd, hh, low], zin.at[k, 0, 0, low], up)
            send(("z", k, "d", 1), zsum.at[zd, hh, high], zin.at[k, 1, 0, high], down)

        def z_step(k, hh, s):
            for i, (way, dev) in enumerate((("u", up), ("d", down))):
                zd = (z + hz - s) % NZ if i == 0 else (z + NZ - hz + s) % NZ
                with_in = every if s > 1 else high if i else low
                arrive(("z", k, way, s), zin.at[k, i, s - 1, with_in], dev)
                total = both(zd, hh, with_in) + zin[k, i, s - 1, with_in].astype(F32)
                zsum[zd, hh, with_in] = total.astype(BF)
                if s == 1:
                    rest = low if i else high
                    zsum[zd, hh, rest] = both(zd, hh, rest).astype(BF)
                send(("z", k, way, s + 1), zsum.at[zd, hh], zin.at[k, i, s], dev)

        def z_end(k, hh):
            arrive(("z", k, "u", hz), zin.at[k, 0, hz - 1], up)
            arrive(("z", k, "d", hz), zin.at[k, 1, hz - 1], down)
            total = both(z, hh, every) + zin[k, 0, hz - 1].astype(F32)
            return total + zin[k, 1, hz - 1].astype(F32)

        zs, dst = core_views(0)
        arrive(("c", 0), dst, other_c)
        z_start(0, 1 - h)
        z_start(1, h)
        for k in range(1, NB):
            zs, dst = core_views(k)
            arrive(("c", k), dst, other_c)

        for s in range(1, max(hx, hz)):
            if s < hz:
                z_step(0, 1 - h, s)
            if s < hx:
                scatter_step("o", o_part, o_in, s)
            if s < hz:
                z_step(1, h, s)
            if s < hx:
                scatter_step("dx", d_part, d_in, s)

        def line_start(name, total, pieces, into):
            spread = None
            for s in range(SEG):
                term = mm(place_of(s), total[:, s * seg_w : (s + 1) * seg_w], TN)
                spread = term if spread is None else spread + term
            pieces[...] = spread.astype(BF).reshape(NY, chunk, seg_w)
            for k in range(1, NY):
                dst_y = (y + k) % NY
                send((name, k), pieces.at[dst_y], into.at[k - 1], at_y(dst_y))

        def line_end(name, pieces, into, result):
            total = pieces[pl.ds(y, 1)].reshape(chunk, seg_w).astype(F32)
            for k in range(1, NY):
                arrive((name, k), into.at[k - 1], at_y((y + k) % NY))
                total = total + into[k - 1].astype(F32)
            total = total.astype(BF)
            for s in range(SEG):
                r, q = iota((chunk, chunk), 0), iota((chunk, chunk), 1)
                back = ((q == r + s * tok) & (r < tok)).astype(BF)
                result[:, s * seg_w : (s + 1) * seg_w] = mm(back, total)[0:tok].astype(BF)

        hout[...] = z_end(0, 1 - h).astype(BF)
        send(("h",), hout, hin, other_h)
        line_start("oy", scatter_end("o", o_part, o_in), oc, oy)
        line_start("xy2", scatter_end("dx", d_part, d_in), xo, xdy)
        total = z_end(1, h)
        line_end("oy", oc, oy, out_ref)
        line_end("xy2", xo, xdy, dx_ref)
        arrive(("h",), hin, other_h)
        total = (total + hin[...].astype(F32)).astype(BF)
        gg_ref[...] = total[0:dr]
        gu_ref[...] = total[dr : 2 * dr]
        eye = (iota((dr, dr), 0) == iota((dr, dr), 1)).astype(BF)
        gd_ref[...] = mm(total[2 * dr : gr], eye, TN).astype(BF)

        for op in sent:
            op.wait_send()
        assert len(ids) <= n_copies

    def vm(shape, dtype=BF):
        return pltpu.VMEM(shape, dtype)

    scratch = [
        vm((d, 2 * ff)), vm((ff, d)),
        vm((chunk, seg_w)), vm((chunk, seg_w)), vm((8, 128), F32),
        vm((NY, chunk, seg_w)), vm((NY, chunk, seg_w)), vm((NY, 8, 128), F32),
        vm((rows, d)), vm((rows, d)), vm((NX, 8, 128), F32), vm((rows, d)),
        vm((rows, d)), vm((rows, d)), vm((2, hx, brow, d)), vm((2, hx, brow, d)),
        vm((NY, chunk, seg_w)), vm((NY, chunk, seg_w)),
        vm((NY - 1, chunk, seg_w)), vm((NY - 1, chunk, seg_w)),
        vm((NC, NZ, NH, gr, ff)), vm((NZ, NH, gr, ff)), vm((NZ, NH, gr, ff)),
        vm((2, 2, hz, gr, ff)), vm((gr, ff)), vm((gr, ff)),
        pltpu.SemaphoreType.DMA((3,)),
        pltpu.SemaphoreType.DMA((n_copies,)),
        pltpu.SemaphoreType.DMA((n_copies,)),
    ]
    vmem, hbm = pl.BlockSpec(memory_space=pltpu.VMEM), pl.BlockSpec(memory_space=pl.ANY)
    return pl.pallas_call(
        kernel,
        out_shape=(
            jax.ShapeDtypeStruct((tok, d), BF),
            jax.ShapeDtypeStruct((tok, d), BF),
            jax.ShapeDtypeStruct((dr, ff), BF),
            jax.ShapeDtypeStruct((dr, ff), BF),
            jax.ShapeDtypeStruct((ff, dr), BF),
        ),
        in_specs=[vmem] * 4 + [hbm] * 3,
        out_specs=(vmem,) * 5,
        scratch_shapes=scratch,
        compiler_params=pltpu.CompilerParams(
            collective_id=0, has_side_effects=True, vmem_limit_bytes=48 * 1024 * 1024
        ),
    )


def local(tokens, routes, route_gates, out_grad, w_gate, w_up, w_down):
    call = build(tokens.shape[0], tokens.shape[1], w_gate.shape[1])
    return call(tokens, routes, route_gates, out_grad, w_gate, w_up, w_down)


def solution(mesh):
    return jax.shard_map(
        local,
        mesh=mesh,
        in_specs=(
            P(("dp", "expert"), None),
            P(("dp", "expert"), None),
            P(("dp", "expert"), None),
            P(("dp", "expert"), None),
            P(None, "expert"),
            P(None, "expert"),
            P("expert", None),
        ),
        out_specs=(
            P(("dp", "expert"), None),
            P(("dp", "expert"), None),
            P("dp", "expert"),
            P("dp", "expert"),
            P("expert", "dp"),
        ),
        check_vma=False,
    )
```

```python
import jax
import jax.numpy as jnp
from jax import lax
from jax.experimental import pallas as pl
from jax.experimental.pallas import tpu as pltpu
from jax.sharding import PartitionSpec as P

NX, NY, NZ, NH, NC = 8, 4, 8, 2, 2
EXPERTS = 4
SEG = 4
NB = 4
BF, F32 = jnp.bfloat16, jnp.float32
NN, NT, TN = (((1,), (0,)), ((), ())), (((1,), (1,)), ((), ())), (((0,), (0,)), ((), ()))


def mm(a, b, dims=NN, precision=None):
    return lax.dot_general(a, b, dims, precision=precision, preferred_element_type=F32)


def iota(shape, dim):
    return lax.broadcasted_iota(jnp.int32, shape, dim)


def split(n, tile):
    return -(-(n // tile) // 2) * tile


def build(tok, d, ff, topk):
    lt, le = tok.bit_length() - 1, EXPERTS.bit_length() - 1
    ly = NY.bit_length() - 1
    seg_w = d // SEG
    chunk = SEG * tok
    brow = NY * tok
    rows = NX * brow
    hx, hz = NX // 2, NZ // 2
    bw, zb = d // NB, NZ // NB
    dr = d // (NZ * NH * NC)
    gr = 3 * dr
    ds = split(d, 128)
    gs = split(gr, 16)
    kb = 512
    n_copies = 9 * NY + 5 * 2 * hx + NB + 2 * 2 * hz + 4

    def kernel(
        tok_hbm, routes_hbm, gates_hbm, og_hbm, wg_hbm, wu_hbm, wd_hbm,
        out_ref, dx_ref, grad_ref,
        tok_ref, routes_ref, gates_ref, og_ref, wgu, wd, xc, dc, gc, xy, dy, gy, xg, dg, gx, sdo,
        o_part, d_part, o_in, d_in, oc, xo, oy, xdy,
        gp, gcin, zsum, zin, hout, hin,
        wsem, ssem, rsem,
    ):
        dp, ei = lax.axis_index("dp"), lax.axis_index("expert")
        x, y = ei // NY, ei % NY
        z, h, c = dp // (NH * NC), (dp // NC) % NH, dp % NC

        def at_x(v):
            return (dp, v * NY + y)

        def at_y(v):
            return (dp, x * NY + v)

        def at_z(v):
            return ((v * NH + h) * NC + c, ei)

        right, left = at_x((x + 1) % NX), at_x((x + NX - 1) % NX)
        up, down = at_z((z + 1) % NZ), at_z((z + NZ - 1) % NZ)
        other_h = ((z * NH + 1 - h) * NC + c, ei)
        other_c = ((z * NH + h) * NC + 1 - c, ei)
        partners = [at_y((y + k) % NY) for k in range(1, NY)]
        partners += [right, left, up, down, other_h, other_c]

        barrier = pltpu.get_barrier_semaphore()
        for p in partners:
            pl.semaphore_signal(barrier, inc=1, device_id=p, device_id_type=pl.DeviceIdType.MESH)

        small = [
            pltpu.make_async_copy(tok_hbm, tok_ref, wsem.at[3]),
            pltpu.make_async_copy(routes_hbm, routes_ref, wsem.at[4]),
            pltpu.make_async_copy(gates_hbm, gates_ref, wsem.at[5]),
            pltpu.make_async_copy(og_hbm, og_ref, wsem.at[6]),
        ]
        for load in small:
            load.start()
        loads = [
            pltpu.make_async_copy(wg_hbm, wgu.at[:, 0:ff], wsem.at[0]),
            pltpu.make_async_copy(wu_hbm, wgu.at[:, ff : 2 * ff], wsem.at[1]),
            pltpu.make_async_copy(wd_hbm, wd, wsem.at[2]),
        ]
        for load in loads:
            load.start()

        sent = []
        ids = {}

        def copy(key, src, dst, dev):
            n = ids.setdefault(key, len(ids))
            return pltpu.make_async_remote_copy(
                src_ref=src, dst_ref=dst, send_sem=ssem.at[n], recv_sem=rsem.at[n],
                device_id=dev, device_id_type=pl.DeviceIdType.MESH,
            )

        def send(key, src, dst, dev):
            op = copy(key, src, dst, dev)
            op.start()
            sent.append(op)

        def arrive(key, dst, dev):
            copy(key, dst, dst, dev).wait_recv()

        def pack(ref):
            total = None
            for s in range(SEG):
                place = (iota((chunk, tok), 0) == iota((chunk, tok), 1) + s * tok).astype(BF)
                term = mm(place, ref[:, s * seg_w : (s + 1) * seg_w])
                total = term if total is None else total + term
            return total.astype(BF)

        small[0].wait()
        xc[...] = pack(tok_ref)
        small[1].wait()
        small[2].wait()
        lane = iota((1, 128), 1)
        line = jnp.zeros((1, 128), F32)
        for k in range(topk):
            for t in range(tok):
                mine = lane == t * EXPERTS + routes_ref[k : k + 1, t : t + 1]
                line = line + jnp.where(mine, gates_ref[k : k + 1, t : t + 1], 0.0)
        gc[...] = jnp.where(iota((8, 128), 0) == y, line, 0.0)

        pl.semaphore_wait(barrier, len(partners))

        for k in range(1, NY):
            send(("yx", k), xc, xy.at[y], at_y((y + k) % NY))
        for k in range(1, NY):
            send(("yg", k), gc, gy.at[y], at_y((y + k) % NY))
        small[3].wait()
        dc[...] = pack(og_ref)
        for k in range(1, NY):
            send(("yd", k), dc, dy.at[y], at_y((y + k) % NY))

        def place_of(s):
            r, q = iota((brow, NY * chunk), 0), iota((brow, NY * chunk), 1)
            return (q == (r >> lt) * chunk + s * tok + (r & (tok - 1))).astype(BF)

        def xrows(v):
            return pl.ds(pl.multiple_of((v % NX) * brow, brow), brow)

        def unpack_to(buf, own, dst):
            buf[pl.ds(y, 1)] = own[...][None]
            all_rows = buf[...].reshape(NY * chunk, seg_w)
            for s in range(SEG):
                dst[xrows(x), s * seg_w : (s + 1) * seg_w] = mm(place_of(s), all_rows).astype(BF)

        def gather_views(name, s):
            buf = {"x": xg, "d": dg}[name]
            r_cols, l_cols = (slice(0, ds), slice(ds, d)) if s == hx else (slice(0, d), slice(0, d))
            return buf, r_cols, l_cols

        def gather_send(name, s):
            buf, rc, lc = gather_views(name, s)
            v = buf.at[xrows(x + NX - s + 1), rc]
            send((name, "r", s), v, v, right)
            v = buf.at[xrows(x + s - 1), lc]
            send((name, "l", s), v, v, left)

        def gather_arrive(name, s):
            buf, rc, lc = gather_views(name, s)
            arrive((name, "r", s), buf.at[xrows(x + NX - s), rc], right)
            arrive((name, "l", s), buf.at[xrows(x + s), lc], left)

        def gate_send(s):
            v = gx.at[(x + NX - s + 1) % NX]
            send(("g", "r", s), v, v, right)
            if s < hx:
                v = gx.at[(x + s - 1) % NX]
                send(("g", "l", s), v, v, left)

        def gate_arrive(s):
            arrive(("g", "r", s), gx.at[(x + NX - s) % NX], right)
            if s < hx:
                arrive(("g", "l", s), gx.at[(x + s) % NX], left)

        for k in range(1, NY):
            arrive(("yx", k), xy.at[(y + NY - k) % NY], at_y((y + k) % NY))
        unpack_to(xy, xc, xg)
        gather_send("x", 1)
        for k in range(1, NY):
            arrive(("yg", k), gy.at[(y + NY - k) % NY], at_y((y + k) % NY))
        gy[pl.ds(y, 1)] = gc[...][None]
        gx[pl.ds(x, 1)] = jnp.sum(gy[...], axis=0, keepdims=True)
        gate_send(1)
        for k in range(1, NY):
            arrive(("yd", k), dy.at[(y + NY - k) % NY], at_y((y + k) % NY))
        unpack_to(dy, dc, dg)
        gather_send("d", 1)
        for s in range(1, hx):
            gather_arrive("x", s)
            gather_send("x", s + 1)
            gate_arrive(s)
            gate_send(s + 1)
            gather_arrive("d", s)
            gather_send("d", s + 1)
        gather_arrive("x", hx)
        gate_arrive(hx)

        expert = ei // (NX * NY // EXPERTS)
        t, q = iota((rows, NX * 8), 0), iota((rows, NX * 8), 1)
        pick = (q == (t >> (lt + ly)) * 8 + ((t >> lt) & (NY - 1))).astype(F32)
        picked = mm(pick, gx[...].reshape(NX * 8, 128), precision=lax.Precision.HIGHEST)
        t, q = iota((rows, 128), 0), iota((rows, 128), 1)
        mine = q == (t & (tok - 1)) * EXPERTS + expert
        gate = jnp.sum(jnp.where(mine, picked, 0.0), axis=1, keepdims=True)

        loads[0].wait()
        loads[1].wait()
        ab = jnp.zeros((rows, 2 * ff), F32)
        for i in range(0, d, kb):
            ab = ab + mm(xg[:, i : i + kb], wgu[i : i + kb, :])
        a, b = ab[:, 0:ff], ab[:, ff : 2 * ff]
        sig = jax.nn.sigmoid(a)
        act = a * sig
        hidden = (act * b).astype(BF)
        loads[2].wait()
        for i in range(0, d, kb):
            o_part[:, i : i + kb] = (mm(hidden, wd[:, i : i + kb]) * gate).astype(BF)

        def scatter_start(name, part, into):
            v = part.at[xrows(x + hx), 0:ds]
            send((name, "r", 1), v, into.at[0, 0, :, 0:ds], right)
            v = part.at[xrows(x + hx), ds:d]
            send((name, "l", 1), v, into.at[1, 0, :, ds:d], left)

        def scatter_step(name, part, into, s):
            for i, (way, dev) in enumerate((("r", right), ("l", left))):
                cols = slice(0, d) if s > 1 else slice(ds, d) if i else slice(0, ds)
                arrive((name, way, s), into.at[i, s - 1, :, cols], dev)
                at = xrows(x + hx - s) if i == 0 else xrows(x + NX - hx + s)
                total = part[at, cols].astype(F32) + into[i, s - 1, :, cols].astype(F32)
                part[at, cols] = total.astype(BF)
                send((name, way, s + 1), part.at[at], into.at[i, s], dev)

        def scatter_end(name, part, into):
            arrive((name, "r", hx), into.at[0, hx - 1], right)
            arrive((name, "l", hx), into.at[1, hx - 1], left)
            total = part[xrows(x), :].astype(F32) + into[0, hx - 1].astype(F32)
            return (total + into[1, hx - 1].astype(F32)).astype(BF)

        scatter_start("o", o_part, o_in)

        gather_arrive("d", hx)
        dh = jnp.zeros((rows, ff), F32)
        for i in range(0, d, kb):
            v = (dg[:, i : i + kb].astype(F32) * gate).astype(BF)
            sdo[:, i : i + kb] = v
            dh = dh + mm(v, wd[:, i : i + kb], NT)
        d_up = (dh * act).astype(BF)
        d_gate = (dh * b * sig * (1.0 + a * (1.0 - sig))).astype(BF)
        dgu = jnp.concatenate([d_gate, d_up], axis=1)

        order = [NB // 2, *(v for k in range(1, NB // 2) for v in (k, NB - k)), 0]

        def core_views(k):
            zs = pl.ds(((z // zb + order[k]) % NB) * zb, zb)
            return zs, gcin.at[zs]

        def grad_block(k):
            block = (z // zb + order[k]) % NB
            cols = pl.ds(pl.multiple_of(block * bw, bw), bw)
            pgu = mm(xg[:, cols], dgu, TN).astype(BF)
            pd = mm(sdo[:, cols], hidden, TN).astype(BF)
            for zz in range(zb):
                for hh in range(NH):
                    for cc in range(NC):
                        at = slice(((zz * NH + hh) * NC + cc) * dr, ((zz * NH + hh) * NC + cc + 1) * dr)
                        gp[cc, block * zb + zz, hh, 0:dr] = pgu[at, 0:ff]
                        gp[cc, block * zb + zz, hh, dr : 2 * dr] = pgu[at, ff : 2 * ff]
                        gp[cc, block * zb + zz, hh, 2 * dr : gr] = pd[at]
            zs, dst = core_views(k)
            send(("c", k), gp.at[1 - c, zs], dst, other_c)

        def core_arrive(k):
            zs, dst = core_views(k)
            arrive(("c", k), dst, other_c)

        def both(zd, hh, at):
            return gp[c, zd, hh, at].astype(F32) + gcin[zd, hh, at].astype(F32)

        every, low, high = slice(0, gr), slice(0, gs), slice(gs, gr)

        def z_start(k, hh):
            zd = (z + hz) % NZ
            zsum[zd, hh] = both(zd, hh, every).astype(BF)
            send(("z", k, "u", 1), zsum.at[zd, hh, low], zin.at[k, 0, 0, low], up)
            send(("z", k, "d", 1), zsum.at[zd, hh, high], zin.at[k, 1, 0, high], down)

        def z_step(k, hh, s):
            for i, (way, dev) in enumerate((("u", up), ("d", down))):
                zd = (z + hz - s) % NZ if i == 0 else (z + NZ - hz + s) % NZ
                with_in = every if s > 1 else high if i else low
                arrive(("z", k, way, s), zin.at[k, i, s - 1, with_in], dev)
                total = both(zd, hh, with_in) + zin[k, i, s - 1, with_in].astype(F32)
                zsum[zd, hh, with_in] = total.astype(BF)
                if s == 1:
                    rest = low if i else high
                    zsum[zd, hh, rest] = both(zd, hh, rest).astype(BF)
                send(("z", k, way, s + 1), zsum.at[zd, hh], zin.at[k, i, s], dev)

        def z_end(k, hh):
            arrive(("z", k, "u", hz), zin.at[k, 0, hz - 1], up)
            arrive(("z", k, "d", hz), zin.at[k, 1, hz - 1], down)
            total = both(z, hh, every) + zin[k, 0, hz - 1].astype(F32)
            return total + zin[k, 1, hz - 1].astype(F32)

        grad_block(0)
        grad_block(1)
        scatter_step("o", o_part, o_in, 1)
        core_arrive(0)
        z_start(0, 1 - h)
        z_start(1, h)
        for k in range(2, NB):
            grad_block(k)
        for i in range(0, d, kb):
            d_part[:, i : i + kb] = mm(dgu, wgu[i : i + kb, :], NT).astype(BF)
        scatter_start("dx", d_part, d_in)
        for k in range(1, NB):
            core_arrive(k)

        for s in range(1, max(hx, hz)):
            if s < hz:
                z_step(0, 1 - h, s)
            if 1 < s < hx:
                scatter_step("o", o_part, o_in, s)
            if s < hz:
                z_step(1, h, s)
            if s < hx:
                scatter_step("dx", d_part, d_in, s)

        def line_start(name, total, pieces, into):
            spread = None
            for s in range(SEG):
                term = mm(place_of(s), total[:, s * seg_w : (s + 1) * seg_w], TN)
                spread = term if spread is None else spread + term
            pieces[...] = spread.astype(BF).reshape(NY, chunk, seg_w)
            for k in range(1, NY):
                dst_y = (y + k) % NY
                send((name, k), pieces.at[dst_y], into.at[k - 1], at_y(dst_y))

        def line_end(name, pieces, into, result):
            total = pieces[pl.ds(y, 1)].reshape(chunk, seg_w).astype(F32)
            for k in range(1, NY):
                arrive((name, k), into.at[k - 1], at_y((y + k) % NY))
                total = total + into[k - 1].astype(F32)
            total = total.astype(BF)
            for s in range(SEG):
                r, q = iota((chunk, chunk), 0), iota((chunk, chunk), 1)
                back = ((q == r + s * tok) & (r < tok)).astype(BF)
                result[:, s * seg_w : (s + 1) * seg_w] = mm(back, total)[0:tok].astype(BF)

        hout[...] = z_end(0, 1 - h).astype(BF)
        send(("h",), hout, hin, other_h)
        line_start("oy", scatter_end("o", o_part, o_in), oc, oy)
        line_start("xy2", scatter_end("dx", d_part, d_in), xo, xdy)
        total = z_end(1, h)
        line_end("oy", oc, oy, out_ref)
        line_end("xy2", xo, xdy, dx_ref)
        arrive(("h",), hin, other_h)
        grad_ref[...] = (total + hin[...].astype(F32)).astype(BF)

        for op in sent:
            op.wait_send()
        assert len(ids) <= n_copies

    def vm(shape, dtype=BF):
        return pltpu.VMEM(shape, dtype)

    scratch = [
        vm((tok, d)), vm((topk, tok), jnp.int32), vm((topk, tok), F32), vm((tok, d)),
        vm((d, 2 * ff)), vm((ff, d)),
        vm((chunk, seg_w)), vm((chunk, seg_w)), vm((8, 128), F32),
        vm((NY, chunk, seg_w)), vm((NY, chunk, seg_w)), vm((NY, 8, 128), F32),
        vm((rows, d)), vm((rows, d)), vm((NX, 8, 128), F32), vm((rows, d)),
        vm((rows, d)), vm((rows, d)), vm((2, hx, brow, d)), vm((2, hx, brow, d)),
        vm((NY, chunk, seg_w)), vm((NY, chunk, seg_w)),
        vm((NY - 1, chunk, seg_w)), vm((NY - 1, chunk, seg_w)),
        vm((NC, NZ, NH, gr, ff)), vm((NZ, NH, gr, ff)), vm((NZ, NH, gr, ff)),
        vm((2, 2, hz, gr, ff)), vm((gr, ff)), vm((gr, ff)),
        pltpu.SemaphoreType.DMA((7,)),
        pltpu.SemaphoreType.DMA((n_copies,)),
        pltpu.SemaphoreType.DMA((n_copies,)),
    ]
    vmem, hbm = pl.BlockSpec(memory_space=pltpu.VMEM), pl.BlockSpec(memory_space=pltpu.HBM)

    def write(a, b, g, a2, b2, g0, g1, g2):
        a2[...] = a[...]
        b2[...] = b[...]
        g0[...] = g[0:dr]
        g1[...] = g[dr : 2 * dr]
        g2[...] = g[2 * dr : gr]

    rows_out = jax.ShapeDtypeStruct((tok, d), BF)
    grad_out = jax.ShapeDtypeStruct((dr, ff), BF)
    main = pl.pallas_call(
        kernel,
        out_shape=(rows_out, rows_out, jax.ShapeDtypeStruct((gr, ff), BF)),
        in_specs=[hbm] * 7,
        out_specs=(vmem,) * 3,
        scratch_shapes=scratch,
        compiler_params=pltpu.CompilerParams(
            collective_id=0, has_side_effects=True, vmem_limit_bytes=60 * 1024 * 1024
        ),
    )
    last = pl.pallas_call(
        write,
        out_shape=(rows_out, rows_out, grad_out, grad_out, grad_out),
        in_specs=[vmem] * 3,
        out_specs=(vmem,) * 5,
        compiler_params=pltpu.CompilerParams(vmem_limit_bytes=60 * 1024 * 1024),
    )
    return main, last


def local(tokens, routes, route_gates, out_grad, w_gate, w_up, w_down):
    main, last = build(tokens.shape[0], tokens.shape[1], w_gate.shape[1], routes.shape[1])
    parts = main(tokens, routes.T, route_gates.T, out_grad, w_gate, w_up, w_down)
    moe_out, token_grad, grad_gate, grad_up, grad_down = last(*parts)
    return moe_out, token_grad, grad_gate, grad_up, grad_down.T


def solution(mesh):
    return jax.shard_map(
        local,
        mesh=mesh,
        in_specs=(
            P(("dp", "expert"), None),
            P(("dp", "expert"), None),
            P(("dp", "expert"), None),
            P(("dp", "expert"), None),
            P(None, "expert"),
            P(None, "expert"),
            P("expert", None),
        ),
        out_specs=(
            P(("dp", "expert"), None),
            P(("dp", "expert"), None),
            P("dp", "expert"),
            P("dp", "expert"),
            P("expert", "dp"),
        ),
        check_vma=False,
    )
```

```python
import jax
import jax.numpy as jnp
from jax import lax
from jax.experimental import pallas as pl
from jax.experimental.pallas import tpu as pltpu
from jax.sharding import PartitionSpec as P

NX, NY, NZ, NH, NC = 8, 4, 8, 2, 2
EXPERTS = 4
SEG = 4
NB = 4
SIDE = 1024
BF, F32 = jnp.bfloat16, jnp.float32
NN, NT, TN = (((1,), (0,)), ((), ())), (((1,), (1,)), ((), ())), (((0,), (0,)), ((), ()))


def mm(a, b, dims=NN, precision=None):
    return lax.dot_general(a, b, dims, precision=precision, preferred_element_type=F32)


def iota(shape, dim):
    return lax.broadcasted_iota(jnp.int32, shape, dim)


def split(n, tile):
    return -(-(n // tile) // 2) * tile


def build(tok, d, ff, topk):
    lt, le = tok.bit_length() - 1, EXPERTS.bit_length() - 1
    ly = NY.bit_length() - 1
    da = d - SIDE
    seg_w, seg_s, seg_o = da // SEG, SIDE // SEG, d // SEG
    side = NX * tok
    chunk = SEG * tok
    brow = NY * tok
    rows = NX * brow
    hx, hz = NX // 2, NZ // 2
    bw, zb = d // NB, NZ // NB
    dr = d // (NZ * NH * NC)
    gr = 3 * dr
    ds, das = split(d, 128), split(da, 128)
    gs = split(gr, 16)
    kb = 512
    n_copies = 11 * NY + NX + 5 * 2 * hx + NB + 2 * 2 * hz + 4

    def kernel(
        tok_hbm, routes_hbm, gates_hbm, og_hbm, wg_hbm, wu_hbm, wd_hbm,
        out_ref, dx_ref, grad_ref,
        tok_ref, routes_ref, gates_ref, og_ref, wgu, wd, xc, dc, bc, bx, bm, by, gc, xy, dy, gy, xg, dg, gx, sdo,
        o_part, d_part, o_in, d_in, oc, xo, oy, xdy,
        gp, gcin, zsum, zin, hout, hin, own,
        wsem, ssem, rsem,
    ):
        dp, ei = lax.axis_index("dp"), lax.axis_index("expert")
        x, y = ei // NY, ei % NY
        z, h, c = dp // (NH * NC), (dp // NC) % NH, dp % NC

        def at_x(v):
            return (dp, v * NY + y)

        def at_y(v):
            return (dp, x * NY + v)

        def at_z(v):
            return ((v * NH + h) * NC + c, ei)

        right, left = at_x((x + 1) % NX), at_x((x + NX - 1) % NX)
        up, down = at_z((z + 1) % NZ), at_z((z + NZ - 1) % NZ)
        other_h = ((z * NH + 1 - h) * NC + c, ei)
        other_c = ((z * NH + h) * NC + 1 - c, ei)
        partners = [at_y((y + k) % NY) for k in range(1, NY)]
        partners += [at_x((x + k) % NX) for k in range(1, NX)]
        partners += [up, down, other_h, other_c]

        barrier = pltpu.get_barrier_semaphore()
        for p in partners:
            pl.semaphore_signal(barrier, inc=1, device_id=p, device_id_type=pl.DeviceIdType.MESH)

        small = [
            pltpu.make_async_copy(tok_hbm, tok_ref, wsem.at[3]),
            pltpu.make_async_copy(routes_hbm, routes_ref, wsem.at[4]),
            pltpu.make_async_copy(gates_hbm, gates_ref, wsem.at[5]),
            pltpu.make_async_copy(og_hbm, og_ref, wsem.at[6]),
        ]
        for load in small:
            load.start()
        loads = [
            pltpu.make_async_copy(wg_hbm, wgu.at[:, 0:ff], wsem.at[0]),
            pltpu.make_async_copy(wu_hbm, wgu.at[:, ff : 2 * ff], wsem.at[1]),
            pltpu.make_async_copy(wd_hbm, wd, wsem.at[2]),
        ]
        for load in loads:
            load.start()

        sent = []
        ids = {}

        def copy(key, src, dst, dev):
            n = ids.setdefault(key, len(ids))
            return pltpu.make_async_remote_copy(
                src_ref=src, dst_ref=dst, send_sem=ssem.at[n], recv_sem=rsem.at[n],
                device_id=dev, device_id_type=pl.DeviceIdType.MESH,
            )

        def send(key, src, dst, dev):
            op = copy(key, src, dst, dev)
            op.start()
            sent.append(op)

        def arrive(key, dst, dev):
            copy(key, dst, dst, dev).wait_recv()

        def pack(ref, start, width):
            total = None
            for s in range(SEG):
                place = (iota((chunk, tok), 0) == iota((chunk, tok), 1) + s * tok).astype(BF)
                term = mm(place, ref[:, start + s * width : start + (s + 1) * width])
                total = term if total is None else total + term
            return total.astype(BF)

        small[0].wait()
        xc[...] = pack(tok_ref, 0, seg_w)
        pl.semaphore_wait(barrier, len(partners))


        for k in range(1, NY):
            send(("yx", k), xc, xy.at[y], at_y((y + k) % NY))
        small[3].wait()
        bc[0:chunk] = pack(tok_ref, da, seg_s)
        bc[chunk : 2 * chunk] = pack(og_ref, da, seg_s)
        for k in range(1, NX):
            send(("bx", k), bc, bx.at[x], at_x((x + k) % NX))
        small[1].wait()
        small[2].wait()
        lane = iota((1, 128), 1)
        line = jnp.zeros((1, 128), F32)
        for k in range(topk):
            for t in range(tok):
                mine = lane == t * EXPERTS + routes_ref[k : k + 1, t : t + 1]
                line = line + jnp.where(mine, gates_ref[k : k + 1, t : t + 1], 0.0)
        gc[...] = jnp.where(iota((8, 128), 0) == y, line, 0.0)

        for k in range(1, NY):
            send(("yg", k), gc, gy.at[y], at_y((y + k) % NY))
        dc[...] = pack(og_ref, 0, seg_w)
        for k in range(1, NY):
            send(("yd", k), dc, dy.at[y], at_y((y + k) % NY))

        def place_of(s):
            r, q = iota((brow, NY * chunk), 0), iota((brow, NY * chunk), 1)
            return (q == (r >> lt) * chunk + s * tok + (r & (tok - 1))).astype(BF)

        def xrows(v):
            return pl.ds(pl.multiple_of((v % NX) * brow, brow), brow)

        def unpack_to(buf, own, dst):
            buf[pl.ds(y, 1)] = own[...][None]
            all_rows = buf[...].reshape(NY * chunk, seg_w)
            for s in range(SEG):
                dst[xrows(x), s * seg_w : (s + 1) * seg_w] = mm(place_of(s), all_rows).astype(BF)

        def gather_views(name, s):
            buf = {"x": xg, "d": dg}[name]
            r_cols, l_cols = (slice(0, das), slice(das, da)) if s == hx else (slice(0, da), slice(0, da))
            return buf, r_cols, l_cols

        def gather_send(name, s):
            buf, rc, lc = gather_views(name, s)
            v = buf.at[xrows(x + NX - s + 1), rc]
            send((name, "r", s), v, v, right)
            v = buf.at[xrows(x + s - 1), lc]
            send((name, "l", s), v, v, left)

        def gather_arrive(name, s):
            buf, rc, lc = gather_views(name, s)
            arrive((name, "r", s), buf.at[xrows(x + NX - s), rc], right)
            arrive((name, "l", s), buf.at[xrows(x + s), lc], left)

        def gate_send(s):
            v = gx.at[(x + NX - s + 1) % NX]
            send(("g", "r", s), v, v, right)
            if s < hx:
                v = gx.at[(x + s - 1) % NX]
                send(("g", "l", s), v, v, left)

        def gate_arrive(s):
            arrive(("g", "r", s), gx.at[(x + NX - s) % NX], right)
            if s < hx:
                arrive(("g", "l", s), gx.at[(x + s) % NX], left)

        for k in range(1, NY):
            arrive(("yx", k), xy.at[(y + NY - k) % NY], at_y((y + k) % NY))
        unpack_to(xy, xc, xg)
        gather_send("x", 1)
        for k in range(1, NY):
            arrive(("yg", k), gy.at[(y + NY - k) % NY], at_y((y + k) % NY))
        gy[pl.ds(y, 1)] = gc[...][None]
        gx[pl.ds(x, 1)] = jnp.sum(gy[...], axis=0, keepdims=True)
        gate_send(1)
        for k in range(1, NY):
            arrive(("yd", k), dy.at[(y + NY - k) % NY], at_y((y + k) % NY))
        unpack_to(dy, dc, dg)
        gather_send("d", 1)

        for k in range(1, NX):
            arrive(("bx", k), bx.at[(x + NX - k) % NX], at_x((x + k) % NX))
        bx[pl.ds(x, 1)] = bc[...][None]
        pieces = bx[...].reshape(NX * 2 * chunk, seg_s)
        for s in range(SEG):
            r, q = iota((2 * side, NX * 2 * chunk), 0), iota((2 * side, NX * 2 * chunk), 1)
            from_x = ((r & (side - 1)) >> lt) * (2 * chunk) + (r >> (side.bit_length() - 1)) * chunk
            take = (q == from_x + s * tok + (r & (tok - 1))).astype(BF)
            bm[:, s * seg_s : (s + 1) * seg_s] = mm(take, pieces).astype(BF)
        for k in range(1, NY):
            send(("by", k), bm, by.at[y], at_y((y + k) % NY))

        for s in range(1, hx):
            gather_arrive("x", s)
            gather_send("x", s + 1)
            gate_arrive(s)
            gate_send(s + 1)
            gather_arrive("d", s)
            gather_send("d", s + 1)

        for k in range(1, NY):
            arrive(("by", k), by.at[(y + NY - k) % NY], at_y((y + k) % NY))
        by[pl.ds(y, 1)] = bm[...][None]
        r, q = iota((rows, rows), 0), iota((rows, rows), 1)
        from_y = ((r >> lt) & (NY - 1)) * side + (r >> (lt + ly)) * tok + (r & (tok - 1))
        turn = (q == from_y).astype(BF)
        xg[:, da:d] = mm(turn, by[:, 0:side].reshape(rows, SIDE)).astype(BF)
        dg[:, da:d] = mm(turn, by[:, side : 2 * side].reshape(rows, SIDE)).astype(BF)
        gather_arrive("x", hx)
        gate_arrive(hx)

        expert = ei // (NX * NY // EXPERTS)
        t, q = iota((rows, NX * 8), 0), iota((rows, NX * 8), 1)
        pick = (q == (t >> (lt + ly)) * 8 + ((t >> lt) & (NY - 1))).astype(F32)
        picked = mm(pick, gx[...].reshape(NX * 8, 128), precision=lax.Precision.HIGHEST)
        t, q = iota((rows, 128), 0), iota((rows, 128), 1)
        mine = q == (t & (tok - 1)) * EXPERTS + expert
        gate = jnp.sum(jnp.where(mine, picked, 0.0), axis=1, keepdims=True)

        loads[0].wait()
        loads[1].wait()
        ab = jnp.zeros((rows, 2 * ff), F32)
        for i in range(0, d, kb):
            ab = ab + mm(xg[:, i : i + kb], wgu[i : i + kb, :])
        a, b = ab[:, 0:ff], ab[:, ff : 2 * ff]
        sig = jax.nn.sigmoid(a)
        act = a * sig
        hidden = (act * b).astype(BF)
        loads[2].wait()
        for i in range(0, d, kb):
            o_part[:, i : i + kb] = (mm(hidden, wd[:, i : i + kb]) * gate).astype(BF)

        def scatter_start(name, part, into):
            v = part.at[xrows(x + hx), 0:ds]
            send((name, "r", 1), v, into.at[0, 0, :, 0:ds], right)
            v = part.at[xrows(x + hx), ds:d]
            send((name, "l", 1), v, into.at[1, 0, :, ds:d], left)

        def scatter_step(name, part, into, s):
            for i, (way, dev) in enumerate((("r", right), ("l", left))):
                cols = slice(0, d) if s > 1 else slice(ds, d) if i else slice(0, ds)
                arrive((name, way, s), into.at[i, s - 1, :, cols], dev)
                at = xrows(x + hx - s) if i == 0 else xrows(x + NX - hx + s)
                total = part[at, cols].astype(F32) + into[i, s - 1, :, cols].astype(F32)
                part[at, cols] = total.astype(BF)
                send((name, way, s + 1), part.at[at], into.at[i, s], dev)

        def scatter_end(name, part, into):
            arrive((name, "r", hx), into.at[0, hx - 1], right)
            arrive((name, "l", hx), into.at[1, hx - 1], left)
            total = part[xrows(x), :].astype(F32) + into[0, hx - 1].astype(F32)
            return (total + into[1, hx - 1].astype(F32)).astype(BF)

        scatter_start("o", o_part, o_in)

        gather_arrive("d", hx)
        dh = jnp.zeros((rows, ff), F32)
        for i in range(0, d, kb):
            v = (dg[:, i : i + kb].astype(F32) * gate).astype(BF)
            sdo[:, i : i + kb] = v
            dh = dh + mm(v, wd[:, i : i + kb], NT)
        d_up = (dh * act).astype(BF)
        d_gate = (dh * b * sig * (1.0 + a * (1.0 - sig))).astype(BF)
        dgu = jnp.concatenate([d_gate, d_up], axis=1)

        order = [NB // 2, *(v for k in range(1, NB // 2) for v in (k, NB - k)), 0]

        def core_views(k):
            zs = pl.ds(((z // zb + order[k]) % NB) * zb, zb)
            return zs, gcin.at[zs]

        def grad_block(k):
            block = (z // zb + order[k]) % NB
            cols = pl.ds(pl.multiple_of(block * bw, bw), bw)
            pgu = mm(xg[:, cols], dgu, TN).astype(BF)
            pd = mm(sdo[:, cols], hidden, TN).astype(BF)
            for zz in range(zb):
                for hh in range(NH):
                    for cc in range(NC):
                        at = slice(((zz * NH + hh) * NC + cc) * dr, ((zz * NH + hh) * NC + cc + 1) * dr)
                        gp[cc, block * zb + zz, hh, 0:dr] = pgu[at, 0:ff]
                        gp[cc, block * zb + zz, hh, dr : 2 * dr] = pgu[at, ff : 2 * ff]
                        gp[cc, block * zb + zz, hh, 2 * dr : gr] = pd[at]
            zs, dst = core_views(k)
            send(("c", k), gp.at[1 - c, zs], dst, other_c)

        def core_arrive(k):
            zs, dst = core_views(k)
            arrive(("c", k), dst, other_c)

        def both(zd, hh, at):
            return gp[c, zd, hh, at].astype(F32) + gcin[zd, hh, at].astype(F32)

        every, low, high = slice(0, gr), slice(0, gs), slice(gs, gr)

        def z_start(k, hh):
            zd = (z + hz) % NZ
            zsum[zd, hh] = both(zd, hh, every).astype(BF)
            send(("z", k, "u", 1), zsum.at[zd, hh, low], zin.at[k, 0, 0, low], up)
            send(("z", k, "d", 1), zsum.at[zd, hh, high], zin.at[k, 1, 0, high], down)

        def z_step(k, hh, s):
            for i, (way, dev) in enumerate((("u", up), ("d", down))):
                zd = (z + hz - s) % NZ if i == 0 else (z + NZ - hz + s) % NZ
                with_in = every if s > 1 else high if i else low
                arrive(("z", k, way, s), zin.at[k, i, s - 1, with_in], dev)
                total = both(zd, hh, with_in) + zin[k, i, s - 1, with_in].astype(F32)
                zsum[zd, hh, with_in] = total.astype(BF)
                if s == 1:
                    rest = low if i else high
                    zsum[zd, hh, rest] = both(zd, hh, rest).astype(BF)
                send(("z", k, way, s + 1), zsum.at[zd, hh], zin.at[k, i, s], dev)

        def z_end(k, hh):
            arrive(("z", k, "u", hz), zin.at[k, 0, hz - 1], up)
            arrive(("z", k, "d", hz), zin.at[k, 1, hz - 1], down)
            total = both(z, hh, every) + zin[k, 0, hz - 1].astype(F32)
            return total + zin[k, 1, hz - 1].astype(F32)

        def line_start(name, total, pieces, into):
            spread = None
            for s in range(SEG):
                term = mm(place_of(s), total[:, s * seg_o : (s + 1) * seg_o], TN)
                spread = term if spread is None else spread + term
            pieces[...] = spread.astype(BF).reshape(NY, chunk, seg_o)
            for k in range(1, NY):
                dst_y = (y + k) % NY
                send((name, k), pieces.at[dst_y], into.at[k - 1], at_y(dst_y))

        def line_end(name, pieces, into, result):
            total = pieces[pl.ds(y, 1)].reshape(chunk, seg_o).astype(F32)
            for k in range(1, NY):
                arrive((name, k), into.at[k - 1], at_y((y + k) % NY))
                total = total + into[k - 1].astype(F32)
            total = total.astype(BF)
            for s in range(SEG):
                r, q = iota((chunk, chunk), 0), iota((chunk, chunk), 1)
                back = ((q == r + s * tok) & (r < tok)).astype(BF)
                result[:, s * seg_o : (s + 1) * seg_o] = mm(back, total)[0:tok].astype(BF)

        def dx_products():
            for i in range(0, d, kb):
                d_part[:, i : i + kb] = mm(dgu, wgu[i : i + kb, :], NT).astype(BF)
            scatter_start("dx", d_part, d_in)

        def h_start():
            hout[...] = z_end(0, 1 - h).astype(BF)
            send(("h",), hout, hin, other_h)

        def own_end():
            own[...] = z_end(1, h)

        def h_end():
            arrive(("h",), hin, other_h)
            grad_ref[...] = (own[...] + hin[...].astype(F32)).astype(BF)

        dx_products()
        grad_block(0)
        grad_block(1)
        scatter_step("o", o_part, o_in, 1)
        core_arrive(0)
        z_start(0, 1 - h)
        z_start(1, h)
        grad_block(2)
        grad_block(3)
        scatter_step("dx", d_part, d_in, 1)
        core_arrive(1)
        core_arrive(2)
        core_arrive(3)
        scatter_step("o", o_part, o_in, 2)
        z_step(0, 1 - h, 1)
        z_step(1, h, 1)
        scatter_step("dx", d_part, d_in, 2)
        z_step(0, 1 - h, 2)
        scatter_step("o", o_part, o_in, 3)
        z_step(1, h, 2)
        scatter_step("dx", d_part, d_in, 3)
        z_step(0, 1 - h, 3)
        z_step(1, h, 3)
        h_start()
        line_start("oy", scatter_end("o", o_part, o_in), oc, oy)
        line_start("xy2", scatter_end("dx", d_part, d_in), xo, xdy)
        own_end()
        line_end("oy", oc, oy, out_ref)
        line_end("xy2", xo, xdy, dx_ref)
        h_end()

        for op in sent:
            op.wait_send()
        assert len(ids) <= n_copies

    def vm(shape, dtype=BF):
        return pltpu.VMEM(shape, dtype)

    scratch = [
        vm((tok, d)), vm((topk, tok), jnp.int32), vm((topk, tok), F32), vm((tok, d)),
        vm((d, 2 * ff)), vm((ff, d)),
        vm((chunk, seg_w)), vm((chunk, seg_w)),
        vm((2 * chunk, seg_s)), vm((NX, 2 * chunk, seg_s)), vm((2 * side, SIDE)), vm((NY, 2 * side, SIDE)),
        vm((8, 128), F32),
        vm((NY, chunk, seg_w)), vm((NY, chunk, seg_w)), vm((NY, 8, 128), F32),
        vm((rows, d)), vm((rows, d)), vm((NX, 8, 128), F32), vm((rows, d)),
        vm((rows, d)), vm((rows, d)), vm((2, hx, brow, d)), vm((2, hx, brow, d)),
        vm((NY, chunk, seg_o)), vm((NY, chunk, seg_o)),
        vm((NY - 1, chunk, seg_o)), vm((NY - 1, chunk, seg_o)),
        vm((NC, NZ, NH, gr, ff)), vm((NZ, NH, gr, ff)), vm((NZ, NH, gr, ff)),
        vm((2, 2, hz, gr, ff)), vm((gr, ff)), vm((gr, ff)), vm((gr, ff), F32),
        pltpu.SemaphoreType.DMA((7,)),
        pltpu.SemaphoreType.DMA((n_copies,)),
        pltpu.SemaphoreType.DMA((n_copies,)),
    ]
    vmem, hbm = pl.BlockSpec(memory_space=pltpu.VMEM), pl.BlockSpec(memory_space=pltpu.HBM)

    def write(a, b, g, a2, b2, g0, g1, g2):
        a2[...] = a[...]
        b2[...] = b[...]
        g0[...] = g[0:dr]
        g1[...] = g[dr : 2 * dr]
        g2[...] = g[2 * dr : gr]

    rows_out = jax.ShapeDtypeStruct((tok, d), BF)
    grad_out = jax.ShapeDtypeStruct((dr, ff), BF)
    main = pl.pallas_call(
        kernel,
        out_shape=(rows_out, rows_out, jax.ShapeDtypeStruct((gr, ff), BF)),
        in_specs=[hbm] * 7,
        out_specs=(vmem,) * 3,
        scratch_shapes=scratch,
        compiler_params=pltpu.CompilerParams(
            collective_id=0, has_side_effects=True, vmem_limit_bytes=60 * 1024 * 1024
        ),
    )
    last = pl.pallas_call(
        write,
        out_shape=(rows_out, rows_out, grad_out, grad_out, grad_out),
        in_specs=[vmem] * 3,
        out_specs=(vmem,) * 5,
        compiler_params=pltpu.CompilerParams(vmem_limit_bytes=60 * 1024 * 1024),
    )
    return main, last


def local(tokens, routes, route_gates, out_grad, w_gate, w_up, w_down):
    main, last = build(tokens.shape[0], tokens.shape[1], w_gate.shape[1], routes.shape[1])
    parts = main(tokens, routes.T, route_gates.T, out_grad, w_gate, w_up, w_down)
    moe_out, token_grad, grad_gate, grad_up, grad_down = last(*parts)
    return moe_out, token_grad, grad_gate, grad_up, grad_down.T


def solution(mesh):
    return jax.shard_map(
        local,
        mesh=mesh,
        in_specs=(
            P(("dp", "expert"), None),
            P(("dp", "expert"), None),
            P(("dp", "expert"), None),
            P(("dp", "expert"), None),
            P(None, "expert"),
            P(None, "expert"),
            P("expert", None),
        ),
        out_specs=(
            P(("dp", "expert"), None),
            P(("dp", "expert"), None),
            P("dp", "expert"),
            P("dp", "expert"),
            P("expert", "dp"),
        ),
        check_vma=False,
    )
```

```python
import jax
import jax.numpy as jnp
from jax import lax
from jax.experimental import pallas as pl
from jax.experimental.pallas import tpu as pltpu
from jax.sharding import PartitionSpec as P

NX, NY, NZ, NH, NC = 8, 4, 8, 2, 2
EXPERTS = 4
SEG = 4
NB = 4
SIDE = 1024
BF, F32 = jnp.bfloat16, jnp.float32
NN, NT, TN = (((1,), (0,)), ((), ())), (((1,), (1,)), ((), ())), (((0,), (0,)), ((), ()))


def mm(a, b, dims=NN, precision=None):
    return lax.dot_general(a, b, dims, precision=precision, preferred_element_type=F32)


def iota(shape, dim):
    return lax.broadcasted_iota(jnp.int32, shape, dim)


def split(n, tile):
    return -(-(n // tile) // 2) * tile


def build(tok, d, ff, topk):
    lt, le = tok.bit_length() - 1, EXPERTS.bit_length() - 1
    ly = NY.bit_length() - 1
    da = d - SIDE
    seg_w, seg_s = da // SEG, SIDE // SEG
    side = NX * tok
    chunk = SEG * tok
    brow = NY * tok
    rows = NX * brow
    hx, hz = NX // 2, NZ // 2
    bw, zb = d // NB, NZ // NB
    dr = d // (NZ * NH * NC)
    gr = 3 * dr
    das = split(da, 128)
    gs = split(gr, 16)
    kb = 512
    n_copies = 13 * NY + 2 * NX + 5 * 2 * hx + NB + 2 * 2 * hz + 4

    def kernel(
        tok_hbm, routes_hbm, gates_hbm, og_hbm, wg_hbm, wu_hbm, wd_hbm,
        out_ref, dx_ref, grad_ref,
        tok_ref, routes_ref, gates_ref, og_ref, wgu, wd, xc, dc, bc, bx, bm, by, gc, xy, dy, gy, xg, dg, gx, sdo,
        o_part, d_part, o_in, d_in, oc, xo, oy, xdy,
        gp, gcin, zsum, zin, hout, hin, own, oside, osin, dside, dsin, sout, sin,
        wsem, ssem, rsem,
    ):
        dp, ei = lax.axis_index("dp"), lax.axis_index("expert")
        x, y = ei // NY, ei % NY
        z, h, c = dp // (NH * NC), (dp // NC) % NH, dp % NC

        def at_x(v):
            return (dp, v * NY + y)

        def at_y(v):
            return (dp, x * NY + v)

        def at_z(v):
            return ((v * NH + h) * NC + c, ei)

        right, left = at_x((x + 1) % NX), at_x((x + NX - 1) % NX)
        up, down = at_z((z + 1) % NZ), at_z((z + NZ - 1) % NZ)
        other_h = ((z * NH + 1 - h) * NC + c, ei)
        other_c = ((z * NH + h) * NC + 1 - c, ei)
        partners = [at_y((y + k) % NY) for k in range(1, NY)]
        partners += [at_x((x + k) % NX) for k in range(1, NX)]
        partners += [up, down, other_h, other_c]

        barrier = pltpu.get_barrier_semaphore()
        for p in partners:
            pl.semaphore_signal(barrier, inc=1, device_id=p, device_id_type=pl.DeviceIdType.MESH)

        small = [
            pltpu.make_async_copy(tok_hbm, tok_ref, wsem.at[3]),
            pltpu.make_async_copy(routes_hbm, routes_ref, wsem.at[4]),
            pltpu.make_async_copy(gates_hbm, gates_ref, wsem.at[5]),
            pltpu.make_async_copy(og_hbm, og_ref, wsem.at[6]),
        ]
        for load in small:
            load.start()
        loads = [
            pltpu.make_async_copy(wg_hbm, wgu.at[:, 0:ff], wsem.at[0]),
            pltpu.make_async_copy(wu_hbm, wgu.at[:, ff : 2 * ff], wsem.at[1]),
            pltpu.make_async_copy(wd_hbm, wd, wsem.at[2]),
        ]
        for load in loads:
            load.start()

        sent = []
        ids = {}

        def copy(key, src, dst, dev):
            n = ids.setdefault(key, len(ids))
            return pltpu.make_async_remote_copy(
                src_ref=src, dst_ref=dst, send_sem=ssem.at[n], recv_sem=rsem.at[n],
                device_id=dev, device_id_type=pl.DeviceIdType.MESH,
            )

        def send(key, src, dst, dev):
            op = copy(key, src, dst, dev)
            op.start()
            sent.append(op)

        def arrive(key, dst, dev):
            copy(key, dst, dst, dev).wait_recv()

        def pack(ref, start, width):
            total = None
            for s in range(SEG):
                place = (iota((chunk, tok), 0) == iota((chunk, tok), 1) + s * tok).astype(BF)
                term = mm(place, ref[:, start + s * width : start + (s + 1) * width])
                total = term if total is None else total + term
            return total.astype(BF)

        small[0].wait()
        xc[...] = pack(tok_ref, 0, seg_w)
        pl.semaphore_wait(barrier, len(partners))


        for k in range(1, NY):
            send(("yx", k), xc, xy.at[y], at_y((y + k) % NY))
        small[3].wait()
        bc[0:chunk] = pack(tok_ref, da, seg_s)
        bc[chunk : 2 * chunk] = pack(og_ref, da, seg_s)
        for k in range(1, NX):
            send(("bx", k), bc, bx.at[x], at_x((x + k) % NX))
        small[1].wait()
        small[2].wait()
        lane = iota((1, 128), 1)
        line = jnp.zeros((1, 128), F32)
        for k in range(topk):
            for t in range(tok):
                mine = lane == t * EXPERTS + routes_ref[k : k + 1, t : t + 1]
                line = line + jnp.where(mine, gates_ref[k : k + 1, t : t + 1], 0.0)
        gc[...] = jnp.where(iota((8, 128), 0) == y, line, 0.0)

        for k in range(1, NY):
            send(("yg", k), gc, gy.at[y], at_y((y + k) % NY))
        dc[...] = pack(og_ref, 0, seg_w)
        for k in range(1, NY):
            send(("yd", k), dc, dy.at[y], at_y((y + k) % NY))

        def place_of(s):
            r, q = iota((brow, NY * chunk), 0), iota((brow, NY * chunk), 1)
            return (q == (r >> lt) * chunk + s * tok + (r & (tok - 1))).astype(BF)

        def xrows(v):
            return pl.ds(pl.multiple_of((v % NX) * brow, brow), brow)

        def unpack_to(buf, own, dst):
            buf[pl.ds(y, 1)] = own[...][None]
            all_rows = buf[...].reshape(NY * chunk, seg_w)
            for s in range(SEG):
                dst[xrows(x), s * seg_w : (s + 1) * seg_w] = mm(place_of(s), all_rows).astype(BF)

        def gather_views(name, s):
            buf = {"x": xg, "d": dg}[name]
            r_cols, l_cols = (slice(0, das), slice(das, da)) if s == hx else (slice(0, da), slice(0, da))
            return buf, r_cols, l_cols

        def gather_send(name, s):
            buf, rc, lc = gather_views(name, s)
            v = buf.at[xrows(x + NX - s + 1), rc]
            send((name, "r", s), v, v, right)
            v = buf.at[xrows(x + s - 1), lc]
            send((name, "l", s), v, v, left)

        def gather_arrive(name, s):
            buf, rc, lc = gather_views(name, s)
            arrive((name, "r", s), buf.at[xrows(x + NX - s), rc], right)
            arrive((name, "l", s), buf.at[xrows(x + s), lc], left)

        def gate_send(s):
            v = gx.at[(x + NX - s + 1) % NX]
            send(("g", "r", s), v, v, right)
            if s < hx:
                v = gx.at[(x + s - 1) % NX]
                send(("g", "l", s), v, v, left)

        def gate_arrive(s):
            arrive(("g", "r", s), gx.at[(x + NX - s) % NX], right)
            if s < hx:
                arrive(("g", "l", s), gx.at[(x + s) % NX], left)

        for k in range(1, NY):
            arrive(("yx", k), xy.at[(y + NY - k) % NY], at_y((y + k) % NY))
        unpack_to(xy, xc, xg)
        gather_send("x", 1)
        for k in range(1, NY):
            arrive(("yg", k), gy.at[(y + NY - k) % NY], at_y((y + k) % NY))
        gy[pl.ds(y, 1)] = gc[...][None]
        gx[pl.ds(x, 1)] = jnp.sum(gy[...], axis=0, keepdims=True)
        gate_send(1)
        for k in range(1, NY):
            arrive(("yd", k), dy.at[(y + NY - k) % NY], at_y((y + k) % NY))
        unpack_to(dy, dc, dg)
        gather_send("d", 1)

        for k in range(1, NX):
            arrive(("bx", k), bx.at[(x + NX - k) % NX], at_x((x + k) % NX))
        bx[pl.ds(x, 1)] = bc[...][None]
        pieces = bx[...].reshape(NX * 2 * chunk, seg_s)
        for s in range(SEG):
            r, q = iota((2 * side, NX * 2 * chunk), 0), iota((2 * side, NX * 2 * chunk), 1)
            from_x = ((r & (side - 1)) >> lt) * (2 * chunk) + (r >> (side.bit_length() - 1)) * chunk
            take = (q == from_x + s * tok + (r & (tok - 1))).astype(BF)
            bm[:, s * seg_s : (s + 1) * seg_s] = mm(take, pieces).astype(BF)
        for k in range(1, NY):
            send(("by", k), bm, by.at[y], at_y((y + k) % NY))

        for s in range(1, hx):
            gather_arrive("x", s)
            gather_send("x", s + 1)
            gate_arrive(s)
            gate_send(s + 1)
            gather_arrive("d", s)
            gather_send("d", s + 1)

        for k in range(1, NY):
            arrive(("by", k), by.at[(y + NY - k) % NY], at_y((y + k) % NY))
        by[pl.ds(y, 1)] = bm[...][None]
        r, q = iota((rows, rows), 0), iota((rows, rows), 1)
        from_y = ((r >> lt) & (NY - 1)) * side + (r >> (lt + ly)) * tok + (r & (tok - 1))
        turn = (q == from_y).astype(BF)
        xg[:, da:d] = mm(turn, by[:, 0:side].reshape(rows, SIDE)).astype(BF)
        dg[:, da:d] = mm(turn, by[:, side : 2 * side].reshape(rows, SIDE)).astype(BF)
        gather_arrive("x", hx)
        gate_arrive(hx)

        expert = ei // (NX * NY // EXPERTS)
        t, q = iota((rows, NX * 8), 0), iota((rows, NX * 8), 1)
        pick = (q == (t >> (lt + ly)) * 8 + ((t >> lt) & (NY - 1))).astype(F32)
        picked = mm(pick, gx[...].reshape(NX * 8, 128), precision=lax.Precision.HIGHEST)
        t, q = iota((rows, 128), 0), iota((rows, 128), 1)
        mine = q == (t & (tok - 1)) * EXPERTS + expert
        gate = jnp.sum(jnp.where(mine, picked, 0.0), axis=1, keepdims=True)

        loads[0].wait()
        loads[1].wait()
        ab = jnp.zeros((rows, 2 * ff), F32)
        for i in range(0, d, kb):
            ab = ab + mm(xg[:, i : i + kb], wgu[i : i + kb, :])
        a, b = ab[:, 0:ff], ab[:, ff : 2 * ff]
        sig = jax.nn.sigmoid(a)
        act = a * sig
        hidden = (act * b).astype(BF)
        loads[2].wait()
        for i in range(0, d, kb):
            o_part[:, i : i + kb] = (mm(hidden, wd[:, i : i + kb]) * gate).astype(BF)

        def scatter_start(name, part, into):
            v = part.at[xrows(x + hx), 0:das]
            send((name, "r", 1), v, into.at[0, 0, :, 0:das], right)
            v = part.at[xrows(x + hx), das:da]
            send((name, "l", 1), v, into.at[1, 0, :, das:da], left)

        def scatter_step(name, part, into, s):
            for i, (way, dev) in enumerate((("r", right), ("l", left))):
                cols = slice(0, da) if s > 1 else slice(das, da) if i else slice(0, das)
                arrive((name, way, s), into.at[i, s - 1, :, cols], dev)
                at = xrows(x + hx - s) if i == 0 else xrows(x + NX - hx + s)
                total = part[at, cols].astype(F32) + into[i, s - 1, :, cols].astype(F32)
                part[at, cols] = total.astype(BF)
                send((name, way, s + 1), part.at[at, 0:da], into.at[i, s], dev)

        def scatter_end(name, part, into):
            arrive((name, "r", hx), into.at[0, hx - 1], right)
            arrive((name, "l", hx), into.at[1, hx - 1], left)
            total = part[xrows(x), 0:da].astype(F32) + into[0, hx - 1].astype(F32)
            return (total + into[1, hx - 1].astype(F32)).astype(BF)

        def turn_rows():
            r, q = iota((rows, rows), 0), iota((rows, rows), 1)
            from_y = ((r >> lt) & (NY - 1)) * side + (r >> (lt + ly)) * tok + (r & (tok - 1))
            return (q == from_y).astype(BF)

        def side_start(name, part, mine, into):
            mine[...] = mm(turn_rows(), part[:, da:d], TN).astype(BF).reshape(NY, side, SIDE)
            for k in range(1, NY):
                to = (y + k) % NY
                send((name, k), mine.at[to], into.at[k - 1], at_y(to))

        scatter_start("o", o_part, o_in)

        gather_arrive("d", hx)
        dh = jnp.zeros((rows, ff), F32)
        for i in range(0, d, kb):
            v = (dg[:, i : i + kb].astype(F32) * gate).astype(BF)
            sdo[:, i : i + kb] = v
            dh = dh + mm(v, wd[:, i : i + kb], NT)
        d_up = (dh * act).astype(BF)
        d_gate = (dh * b * sig * (1.0 + a * (1.0 - sig))).astype(BF)
        dgu = jnp.concatenate([d_gate, d_up], axis=1)

        order = [NB // 2, *(v for k in range(1, NB // 2) for v in (k, NB - k)), 0]

        def core_views(k):
            zs = pl.ds(((z // zb + order[k]) % NB) * zb, zb)
            return zs, gcin.at[zs]

        def grad_block(k):
            block = (z // zb + order[k]) % NB
            cols = pl.ds(pl.multiple_of(block * bw, bw), bw)
            pgu = mm(xg[:, cols], dgu, TN).astype(BF)
            pd = mm(sdo[:, cols], hidden, TN).astype(BF)
            for zz in range(zb):
                for hh in range(NH):
                    for cc in range(NC):
                        at = slice(((zz * NH + hh) * NC + cc) * dr, ((zz * NH + hh) * NC + cc + 1) * dr)
                        gp[cc, block * zb + zz, hh, 0:dr] = pgu[at, 0:ff]
                        gp[cc, block * zb + zz, hh, dr : 2 * dr] = pgu[at, ff : 2 * ff]
                        gp[cc, block * zb + zz, hh, 2 * dr : gr] = pd[at]
            zs, dst = core_views(k)
            send(("c", k), gp.at[1 - c, zs], dst, other_c)

        def core_arrive(k):
            zs, dst = core_views(k)
            arrive(("c", k), dst, other_c)

        def both(zd, hh, at):
            return gp[c, zd, hh, at].astype(F32) + gcin[zd, hh, at].astype(F32)

        every, low, high = slice(0, gr), slice(0, gs), slice(gs, gr)

        def z_start(k, hh):
            zd = (z + hz) % NZ
            zsum[zd, hh] = both(zd, hh, every).astype(BF)
            send(("z", k, "u", 1), zsum.at[zd, hh, low], zin.at[k, 0, 0, low], up)
            send(("z", k, "d", 1), zsum.at[zd, hh, high], zin.at[k, 1, 0, high], down)

        def z_step(k, hh, s):
            for i, (way, dev) in enumerate((("u", up), ("d", down))):
                zd = (z + hz - s) % NZ if i == 0 else (z + NZ - hz + s) % NZ
                with_in = every if s > 1 else high if i else low
                arrive(("z", k, way, s), zin.at[k, i, s - 1, with_in], dev)
                total = both(zd, hh, with_in) + zin[k, i, s - 1, with_in].astype(F32)
                zsum[zd, hh, with_in] = total.astype(BF)
                if s == 1:
                    rest = low if i else high
                    zsum[zd, hh, rest] = both(zd, hh, rest).astype(BF)
                send(("z", k, way, s + 1), zsum.at[zd, hh], zin.at[k, i, s], dev)

        def z_end(k, hh):
            arrive(("z", k, "u", hz), zin.at[k, 0, hz - 1], up)
            arrive(("z", k, "d", hz), zin.at[k, 1, hz - 1], down)
            total = both(z, hh, every) + zin[k, 0, hz - 1].astype(F32)
            return total + zin[k, 1, hz - 1].astype(F32)

        def line_start(name, total, pieces, into):
            spread = None
            for s in range(SEG):
                term = mm(place_of(s), total[:, s * seg_w : (s + 1) * seg_w], TN)
                spread = term if spread is None else spread + term
            pieces[...] = spread.astype(BF).reshape(NY, chunk, seg_w)
            for k in range(1, NY):
                dst_y = (y + k) % NY
                send((name, k), pieces.at[dst_y], into.at[k - 1], at_y(dst_y))

        def line_end(name, pieces, into, result):
            total = pieces[pl.ds(y, 1)].reshape(chunk, seg_w).astype(F32)
            for k in range(1, NY):
                arrive((name, k), into.at[k - 1], at_y((y + k) % NY))
                total = total + into[k - 1].astype(F32)
            unstack(total.astype(BF), 0, seg_w, result)

        def unstack(total, start, width, result):
            for s in range(SEG):
                r, q = iota((chunk, chunk), 0), iota((chunk, chunk), 1)
                back = ((q == r + s * tok) & (r < tok)).astype(BF)
                result[:, start + s * width : start + (s + 1) * width] = mm(back, total)[0:tok].astype(BF)

        def side_turn():
            for i, (name, mine, into) in enumerate((("os", oside, osin), ("ds", dside, dsin))):
                total = mine[pl.ds(y, 1)].reshape(side, SIDE).astype(F32)
                for k in range(1, NY):
                    arrive((name, k), into.at[k - 1], at_y((y + k) % NY))
                    total = total + into[k - 1].astype(F32)
                total = total.astype(BF)
                spread = None
                for s in range(SEG):
                    r, q = iota((NX * chunk, side), 0), iota((NX * chunk, side), 1)
                    take = (r == (q >> lt) * chunk + s * tok + (q & (tok - 1))).astype(BF)
                    term = mm(take, total[:, s * seg_s : (s + 1) * seg_s])
                    spread = term if spread is None else spread + term
                sout[:, i * chunk : (i + 1) * chunk] = spread.astype(BF).reshape(NX, chunk, seg_s)
            for k in range(1, NX):
                to = (x + k) % NX
                send(("sx", k), sout.at[to], sin.at[k - 1], at_x(to))

        def side_end():
            total = sout[pl.ds(x, 1)].reshape(2 * chunk, seg_s).astype(F32)
            for k in range(1, NX):
                arrive(("sx", k), sin.at[k - 1], at_x((x + k) % NX))
                total = total + sin[k - 1].astype(F32)
            total = total.astype(BF)
            unstack(total[0:chunk], da, seg_s, out_ref)
            unstack(total[chunk : 2 * chunk], da, seg_s, dx_ref)

        def dx_products():
            for i in range(0, d, kb):
                d_part[:, i : i + kb] = mm(dgu, wgu[i : i + kb, :], NT).astype(BF)
            scatter_start("dx", d_part, d_in)

        def h_start():
            hout[...] = z_end(0, 1 - h).astype(BF)
            send(("h",), hout, hin, other_h)

        def own_end():
            own[...] = z_end(1, h)

        def h_end():
            arrive(("h",), hin, other_h)
            grad_ref[...] = (own[...] + hin[...].astype(F32)).astype(BF)

        side_start("os", o_part, oside, osin)
        dx_products()
        grad_block(0)
        grad_block(1)
        scatter_step("o", o_part, o_in, 1)
        core_arrive(0)
        z_start(0, 1 - h)
        z_start(1, h)
        side_start("ds", d_part, dside, dsin)
        grad_block(2)
        grad_block(3)
        scatter_step("dx", d_part, d_in, 1)
        core_arrive(1)
        core_arrive(2)
        core_arrive(3)
        scatter_step("o", o_part, o_in, 2)
        z_step(0, 1 - h, 1)
        z_step(1, h, 1)
        scatter_step("dx", d_part, d_in, 2)
        z_step(0, 1 - h, 2)
        scatter_step("o", o_part, o_in, 3)
        z_step(0, 1 - h, 3)
        z_step(1, h, 2)
        scatter_step("dx", d_part, d_in, 3)
        h_start()
        line_start("oy", scatter_end("o", o_part, o_in), oc, oy)
        side_turn()
        z_step(1, h, 3)
        line_start("xy2", scatter_end("dx", d_part, d_in), xo, xdy)
        own_end()
        line_end("oy", oc, oy, out_ref)
        line_end("xy2", xo, xdy, dx_ref)
        side_end()
        h_end()

        for op in sent:
            op.wait_send()
        assert len(ids) <= n_copies

    def vm(shape, dtype=BF):
        return pltpu.VMEM(shape, dtype)

    scratch = [
        vm((tok, d)), vm((topk, tok), jnp.int32), vm((topk, tok), F32), vm((tok, d)),
        vm((d, 2 * ff)), vm((ff, d)),
        vm((chunk, seg_w)), vm((chunk, seg_w)),
        vm((2 * chunk, seg_s)), vm((NX, 2 * chunk, seg_s)), vm((2 * side, SIDE)), vm((NY, 2 * side, SIDE)),
        vm((8, 128), F32),
        vm((NY, chunk, seg_w)), vm((NY, chunk, seg_w)), vm((NY, 8, 128), F32),
        vm((rows, d)), vm((rows, d)), vm((NX, 8, 128), F32), vm((rows, d)),
        vm((rows, d)), vm((rows, d)), vm((2, hx, brow, da)), vm((2, hx, brow, da)),
        vm((NY, chunk, seg_w)), vm((NY, chunk, seg_w)),
        vm((NY - 1, chunk, seg_w)), vm((NY - 1, chunk, seg_w)),
        vm((NC, NZ, NH, gr, ff)), vm((NZ, NH, gr, ff)), vm((NZ, NH, gr, ff)),
        vm((2, 2, hz, gr, ff)), vm((gr, ff)), vm((gr, ff)), vm((gr, ff), F32),
        vm((NY, side, SIDE)), vm((NY - 1, side, SIDE)), vm((NY, side, SIDE)), vm((NY - 1, side, SIDE)),
        vm((NX, 2 * chunk, seg_s)), vm((NX - 1, 2 * chunk, seg_s)),
        pltpu.SemaphoreType.DMA((7,)),
        pltpu.SemaphoreType.DMA((n_copies,)),
        pltpu.SemaphoreType.DMA((n_copies,)),
    ]
    vmem, hbm = pl.BlockSpec(memory_space=pltpu.VMEM), pl.BlockSpec(memory_space=pltpu.HBM)

    def write(a, b, g, a2, b2, g0, g1, g2):
        a2[...] = a[...]
        b2[...] = b[...]
        g0[...] = g[0:dr]
        g1[...] = g[dr : 2 * dr]
        g2[...] = g[2 * dr : gr]

    rows_out = jax.ShapeDtypeStruct((tok, d), BF)
    grad_out = jax.ShapeDtypeStruct((dr, ff), BF)
    main = pl.pallas_call(
        kernel,
        out_shape=(rows_out, rows_out, jax.ShapeDtypeStruct((gr, ff), BF)),
        in_specs=[hbm] * 7,
        out_specs=(vmem,) * 3,
        scratch_shapes=scratch,
        compiler_params=pltpu.CompilerParams(
            collective_id=0, has_side_effects=True, vmem_limit_bytes=60 * 1024 * 1024
        ),
    )
    last = pl.pallas_call(
        write,
        out_shape=(rows_out, rows_out, grad_out, grad_out, grad_out),
        in_specs=[vmem] * 3,
        out_specs=(vmem,) * 5,
        compiler_params=pltpu.CompilerParams(vmem_limit_bytes=60 * 1024 * 1024),
    )
    return main, last


def local(tokens, routes, route_gates, out_grad, w_gate, w_up, w_down):
    main, last = build(tokens.shape[0], tokens.shape[1], w_gate.shape[1], routes.shape[1])
    parts = main(tokens, routes.T, route_gates.T, out_grad, w_gate, w_up, w_down)
    moe_out, token_grad, grad_gate, grad_up, grad_down = last(*parts)
    return moe_out, token_grad, grad_gate, grad_up, grad_down.T


def solution(mesh):
    return jax.shard_map(
        local,
        mesh=mesh,
        in_specs=(
            P(("dp", "expert"), None),
            P(("dp", "expert"), None),
            P(("dp", "expert"), None),
            P(("dp", "expert"), None),
            P(None, "expert"),
            P(None, "expert"),
            P("expert", None),
        ),
        out_specs=(
            P(("dp", "expert"), None),
            P(("dp", "expert"), None),
            P("dp", "expert"),
            P("dp", "expert"),
            P("expert", "dp"),
        ),
        check_vma=False,
    )
```
